512 devices in a mesh: rep: 32 (over x, y), tp: 16 (over z, core).
Axes of the slice: x: 4, y: 8, z: 8, core: 2. Of those that a mesh axis runs over, the one named last changes fastest.
Arguments:
- hidden: bfloat16 [8192, 53248], P('rep', 'tp'), parts along dimension 0, may hold values from -6 to 6
- codes: bfloat16 [53248, 512], P('tp'), may hold values from -8 to 7, as said below
- scales: float32 [416, 512], P('tp'), may hold values from 0.0003 to 0.003
- sign_bits: int32 [53248], P('tp'), may hold values 0 or 1
Outputs:
- projected: bfloat16 [8192, 512], P(('rep', 'tp')), parts along dimension 0
The draws below stay inside these ranges and needn't reach their ends.
There are 32 independent parts, one for each index of `rep`. The reference program is written for one: setup_inputs(seed, part) draws one part's arguments, and reference() takes and returns one part's arrays. A program takes and returns all parts, laid end to end along the dimension named above; an argument that names none is the same for every part. Nothing has to cross between parts.
Inputs may be any that keep to these rules, and one draw needn't show every extreme that they name: `codes`: whole numbers, the 16 levels of a signed 4-bit code.
All inputs are finite; a program needn't handle non-finite values. No bound on the sum of `sign_bits` on one device may be relied on, other than what follows from the above.
Results may differ from the reference program's by a relative error of at most 0.0064.
Values may be sent and summed in bfloat16 or wider, within the bound.
No kernel may reach another device: no remote copies, remote signals or barrier semaphores. Data moves between devices by JAX's collectives and lax.ppermute only.
A program may use at most 64 MiB of HBM per device.

```python
import math
import jax
import jax.numpy as jnp
from jax import lax

FF = 53248
D_OUT = 512
ROWS = 256
N_TP = 16


def draw_codes(key, part):
    key = jax.random.fold_in(key, 7)
    levels = jax.random.randint(key, (FF, D_OUT), -8, 8)
    return levels.astype(jnp.float32).astype(jnp.bfloat16)


def place_ends(array, own_key, low, high):
    extent = array.shape
    spot = [jax.random.randint(jax.random.fold_in(own_key, axis), (), 0, extent[axis]) for axis in range(len(extent))]
    array = array.at[tuple(spot)].set(low)
    longest = extent.index(max(extent))
    spot[longest] = (spot[longest] + 1) % extent[longest]
    return array.at[tuple(spot)].set(high)


def steps_of(own_key, extent, shards, low, largest):
    gain = 1.0
    for axis_at, blocks in shards:
        draws = jax.random.uniform(jax.random.fold_in(jax.random.fold_in(own_key, 6), axis_at), (blocks,), jnp.float32, low / len(shards), largest / len(shards))
        gain = gain * jnp.repeat(jnp.exp(draws), extent[axis_at] // blocks).reshape((-1,) + (1,) * (len(extent) - 1 - axis_at))
    return gain


def noise(key, extent, spread, reach, pieces=(), kind=jnp.bfloat16):
    result = jax.random.normal(key, extent, jnp.float32) * spread
    if len(pieces) > 0:
        result = steps_of(key, extent, pieces, -0.22, 0.18) * result
    return jnp.clip(result, min=-reach, max=reach).astype(kind)


def setup_inputs(seed: int = 0, part: int = 0) -> dict:
    key_of = jax.random.split(jax.random.key(seed), 5)
    part_keys = jax.random.split(jax.random.fold_in(key_of[4], part), 5)
    return {
        "hidden": noise(part_keys[0], (ROWS, FF), 1.0, 6.0, ((1, 16),)),
        "codes": draw_codes(jax.random.fold_in(key_of[4], 71), part),
        "scales": jnp.clip(jnp.exp(math.log(0.003) - 2.3025851 * jax.random.uniform(key_of[2], (FF // 128, D_OUT), jnp.float32) ** steps_of(key_of[2], (FF // 128, D_OUT), ((0, 16),), -0.2, 0.2)), 0.0003, 0.003),
        "sign_bits": place_ends((jax.random.randint(key_of[3], (FF,), 0, 2) < 1).astype(jnp.int32), jax.random.fold_in(key_of[3], 1), 0, 1),
    }


def sylvester(matrix_size):
    indices = jnp.arange(matrix_size, dtype=jnp.int32)
    common = jnp.bitwise_and(indices[:, None], indices[None, :])
    parity = jnp.zeros((matrix_size, matrix_size), jnp.int32)
    for place in range(matrix_size.bit_length() - 1):
        parity = parity + jnp.bitwise_and(jnp.right_shift(common, place), 1)
    return 1.0 - 2.0 * jnp.bitwise_and(parity, 1).astype(jnp.float32)

def reference(hidden, codes, scales, sign_bits):
    row_count = hidden.shape[0]
    signed = jnp.where(sign_bits[None, :] == 1, hidden, -hidden)
    table = sylvester(256).astype(jnp.bfloat16)
    turned = jnp.dot(signed.reshape(-1, 256), table, preferred_element_type=jnp.float32) * 0.0625
    turned = turned.astype(jnp.bfloat16)
    mixing_table = sylvester(N_TP)
    grouped = turned.astype(jnp.float32).reshape(row_count, N_TP, FF // N_TP)
    rotated = jnp.einsum('pq,rqw->rpw', mixing_table, grouped, precision=lax.Precision.HIGHEST) / math.sqrt(N_TP)
    rotated = rotated.reshape(row_count, FF).astype(jnp.bfloat16)
    weight = codes.astype(jnp.float32).reshape(FF // 128, 128, D_OUT) * scales[:, None, :]
    weight = weight.reshape(FF, D_OUT).astype(jnp.bfloat16)
    return jnp.dot(rotated, weight, preferred_element_type=jnp.float32).astype(jnp.bfloat16)
```

```python
import functools

import jax
import jax.numpy as jnp
from jax import lax
from jax.experimental import pallas as pl
from jax.experimental.pallas import tpu as pltpu
from jax.sharding import Mesh, PartitionSpec as P

BF16 = jnp.bfloat16
F32 = jnp.float32
TURN = 256
GROUP = 128


def sylvester(matrix_size):
    indices = jnp.arange(matrix_size, dtype=jnp.int32)
    common = jnp.bitwise_and(indices[:, None], indices[None, :])
    parity = jnp.zeros((matrix_size, matrix_size), jnp.int32)
    for place in range(matrix_size.bit_length() - 1):
        parity = parity + jnp.bitwise_and(jnp.right_shift(common, place), 1)
    return 1.0 - 2.0 * jnp.bitwise_and(parity, 1).astype(F32)


def parity_sign(a, b, places):
    common = jnp.bitwise_and(a, b)
    parity = functools.reduce(
        jnp.bitwise_xor, [jnp.right_shift(common, place) for place in range(places)]
    )
    return 1.0 - 2.0 * jnp.bitwise_and(parity, 1).astype(F32)


def turn_kernel(hidden_ref, sign_ref, table_ref, out_ref):
    rows, width = hidden_ref.shape
    half = width // 2
    table = table_ref[...]
    for block in range(width // TURN):
        low = block * TURN
        sign = sign_ref[:, low : low + TURN]
        signed = hidden_ref[:, low : low + TURN] * sign
        turned = jnp.dot(signed, table, preferred_element_type=F32).astype(BF16)
        for piece in range(TURN // 128):
            at = low + piece * 128
            part, inside = at // half, at % half
            value = turned[:, piece * 128 : (piece + 1) * 128]
            for copy in range(2):
                out_ref[2 * part + copy, :, inside : inside + 128] = value


def turn(hidden, sign_bits):
    rows, width = hidden.shape
    sign = (2 * sign_bits - 1).astype(BF16)[None, :]
    table = (sylvester(TURN) * (1.0 / 16.0)).astype(BF16)
    return pl.pallas_call(
        turn_kernel,
        out_shape=jax.ShapeDtypeStruct((4, rows, width // 2), BF16),
        cost_estimate=pl.CostEstimate(
            flops=2 * rows * width * TURN, bytes_accessed=10 * rows * width, transcendentals=0
        ),
        compiler_params=pltpu.CompilerParams(vmem_limit_bytes=40 * 1024 * 1024),
    )(hidden, sign, table)


def weight_share(codes, scales, row_at, row_count, col_at, col_count):
    code = lax.dynamic_slice(codes, (row_at, col_at), (row_count, col_count)).astype(F32)
    first = row_at // GROUP
    last = scales.shape[0] - 1
    spot = lax.broadcasted_iota(jnp.int32, (row_count, 1), 0) + row_at
    scale = None
    for step in range((row_count - 1) // GROUP + 2):
        line = lax.dynamic_slice(scales, (jnp.minimum(first + step, last), col_at), (1, col_count))
        scale = line if scale is None else jnp.where(spot // GROUP >= first + step, line, scale)
    return (code * scale).astype(BF16)


def per_device(hidden, codes, scales, sign_bits):
    row_count, local_width = hidden.shape
    out_width = codes.shape[1]
    x_count, y_count = lax.axis_size("x"), lax.axis_size("y")
    z_count, core_count = lax.axis_size("z"), lax.axis_size("core")
    x, y, z, core = (lax.axis_index(name) for name in ("x", "y", "z", "core"))
    part, side = x // 2, x % 2
    half_width, half_out = local_width // 2, out_width // 2
    share = half_width // y_count

    turned = turn(hidden, sign_bits)
    mine = lax.all_to_all(turned, "x", 0, 0, tiled=True)

    weight = weight_share(
        codes, scales, part * half_width + y * share, share, side * half_out, half_out
    )
    other = lax.ppermute(weight, "core", [(0, 1), (1, 0)])
    paired = jnp.where(core == 0, weight.astype(F32), -weight.astype(F32)) + other.astype(F32)
    paired = (paired * 0.5).astype(BF16)
    chips = lax.all_gather(paired, "z")
    signs = parity_sign(jnp.arange(z_count), z, 3) * 0.5
    mixed = jnp.sum(chips.astype(F32) * signs[:, None, None], axis=0).astype(BF16)
    mixed = lax.all_gather(mixed, "y", tiled=True)

    part_sum = jnp.dot(
        mine.reshape(x_count * row_count, half_width), mixed, preferred_element_type=F32
    )
    out_rows = row_count // (z_count * core_count)
    part_sum = part_sum.reshape(x_count, z_count, core_count, out_rows, half_out)
    first, second = part_sum[:, :, 0], part_sum[:, :, 1]
    keep = jnp.where(core == 0, first, second)
    give = jnp.where(core == 0, second, first).astype(BF16)
    got = lax.ppermute(give, "core", [(0, 1), (1, 0)])
    chip_sum = (keep + got.astype(F32)).astype(BF16)
    chip_sum = chip_sum.reshape(x_count * z_count, out_rows, half_out)
    parts = lax.all_to_all(chip_sum, ("x", "z"), 0, 0, tiled=True)
    parts = parts.reshape(2, 2, z_count, out_rows, half_out).astype(F32)
    total = jnp.sum(parts, axis=(0, 2))
    return jnp.concatenate([total[0], total[1]], axis=-1).astype(BF16)


def solution(mesh):
    devices = mesh.devices.reshape(4, 8, 8, 2)
    grid = Mesh(devices, ("x", "y", "z", "core"))
    rep, tp = ("x", "y"), ("z", "core")
    return jax.shard_map(
        per_device,
        mesh=grid,
        in_specs=(P(rep, tp), P(tp, None), P(tp, None), P(tp)),
        out_specs=P(rep + tp, None),
        check_vma=False,
    )
```

```python
import jax
import jax.numpy as jnp
from jax import lax
from jax.experimental import pallas as pl
from jax.experimental.pallas import tpu as pltpu
from jax.sharding import Mesh, PartitionSpec as P

BF16 = jnp.bfloat16
F32 = jnp.float32
TURN = 256
GROUP = 128
LANES = 128
STEP = 16
PARTS, SIDES = 2, 2


def sylvester(matrix_size):
    indices = jnp.arange(matrix_size, dtype=jnp.int32)
    common = jnp.bitwise_and(indices[:, None], indices[None, :])
    parity = jnp.zeros((matrix_size, matrix_size), jnp.int32)
    for place in range(matrix_size.bit_length() - 1):
        parity = parity + jnp.bitwise_and(jnp.right_shift(common, place), 1)
    return 1.0 - 2.0 * jnp.bitwise_and(parity, 1).astype(F32)


def params(mib):
    return pltpu.CompilerParams(vmem_limit_bytes=mib * 1024 * 1024)


def weight_kernel(rows, padded, codes_ref, scales_ref, out_ref, code_vmem, sem):
    x, y = lax.axis_index("x"), lax.axis_index("y")
    share = (x // SIDES) * lax.axis_size("y") + y
    low = pl.multiple_of((x % SIDES) * (2 * LANES), 2 * LANES)
    copy = pltpu.make_async_copy(
        codes_ref.at[pl.ds(pl.multiple_of(share * rows, STEP), rows), pl.ds(low, 2 * LANES)],
        code_vmem,
        sem,
    )
    copy.start()
    out_ref[2 * rows :] = jnp.zeros((padded - 2 * rows, LANES), BF16)
    copy.wait()
    for step in range(rows // STEP):
        group = (share * (rows // STEP) + step) // (GROUP // STEP)
        scale = scales_ref[pl.ds(group, 1), pl.ds(low, 2 * LANES)]
        value = code_vmem[step * STEP : (step + 1) * STEP].astype(F32) * scale
        value = value.astype(BF16)
        for side in range(2):
            at = side * rows + step * STEP
            out_ref[at : at + STEP] = value[:, side * LANES : (side + 1) * LANES]


def weight_share(codes, scales, rows, padded):
    return pl.pallas_call(
        lambda *refs: weight_kernel(rows, padded, *refs),
        out_shape=jax.ShapeDtypeStruct((padded, LANES), BF16),
        in_specs=[
            pl.BlockSpec(memory_space=pl.ANY),
            pl.BlockSpec(memory_space=pltpu.VMEM),
        ],
        scratch_shapes=[pltpu.VMEM((rows, 2 * LANES), BF16), pltpu.SemaphoreType.DMA],
        cost_estimate=pl.CostEstimate(
            flops=2 * rows * LANES, bytes_accessed=8 * rows * LANES, transcendentals=0
        ),
        compiler_params=params(56),
    )(codes, scales)


def mix_kernel(count, in_ref, out_ref):
    rows = in_ref.shape[0] // count
    for low in range(0, rows, STEP):
        blocks = [
            in_ref[p * rows + low : p * rows + low + STEP].astype(F32) for p in range(count)
        ]
        stride = 1
        while stride < count:
            for p in range(count):
                if not p & stride:
                    a, b = blocks[p], blocks[p + stride]
                    blocks[p], blocks[p + stride] = a + b, a - b
            stride *= 2
        for q in range(count):
            value = (blocks[q] * (count**-0.5)).astype(BF16)
            for y in range(out_ref.shape[0]):
                out_ref[y, q, low : low + STEP] = value


def mix(parts, tp_count, y_count):
    rows = parts.shape[0] // tp_count
    return pl.pallas_call(
        lambda *refs: mix_kernel(tp_count, *refs),
        out_shape=jax.ShapeDtypeStruct((y_count, tp_count, rows, LANES), BF16),
        cost_estimate=pl.CostEstimate(
            flops=8 * parts.size, bytes_accessed=20 * parts.size, transcendentals=0
        ),
        compiler_params=params(24),
    )(parts)


def turn_kernel(hidden_ref, bits_ref, table_ref, same_ref, other_ref):
    rows, width = hidden_ref.shape
    half = width // PARTS
    own = lax.axis_index("x") // SIDES
    table = table_ref[...]
    for keep in range(PARTS):

        @pl.when(own == keep)
        def _(keep=keep):
            for low in range(0, width, TURN):
                hidden = hidden_ref[:, low : low + TURN]
                plus = bits_ref[:, low : low + TURN] == 1
                signed = hidden * jnp.where(plus, 1.0, -1.0).astype(BF16)
                turned = jnp.dot(signed, table, preferred_element_type=F32).astype(BF16)
                for piece in range(0, TURN, LANES):
                    part, inside = divmod(low + piece, half)
                    out_ref = same_ref if part == keep else other_ref
                    out_ref[:, inside : inside + LANES] = turned[:, piece : piece + LANES]


def turn(hidden, sign_bits):
    rows, width = hidden.shape
    table = (sylvester(TURN) * (1.0 / 16.0)).astype(BF16)
    half = jax.ShapeDtypeStruct((rows, width // PARTS), BF16)
    return pl.pallas_call(
        turn_kernel,
        out_shape=(half, half),
        cost_estimate=pl.CostEstimate(
            flops=2 * rows * width * TURN, bytes_accessed=4 * rows * width, transcendentals=0
        ),
        compiler_params=params(24),
    )(hidden, sign_bits.reshape(1, width), table)


def project_kernel(rows, act0, act1, act2, act3, mixed_ref, out_ref, weight_vmem):
    for y in range(mixed_ref.shape[0]):
        for side in range(2):
            weight_vmem[y * rows : (y + 1) * rows, side * LANES : (side + 1) * LANES] = mixed_ref[
                y, side * rows : (side + 1) * rows
            ]
    x = lax.axis_index("x")
    for flip, act_ref in enumerate((act0, act1, act2, act3)):
        value = jnp.dot(act_ref[...], weight_vmem[...], preferred_element_type=F32)
        out_ref[jnp.bitwise_xor(x, flip)] = value.astype(BF16)


def project(acts, mixed, rows):
    count, half = acts[0].shape
    return pl.pallas_call(
        lambda *refs: project_kernel(rows, *refs),
        out_shape=jax.ShapeDtypeStruct((len(acts), count, 2 * LANES), BF16),
        scratch_shapes=[pltpu.VMEM((half, 2 * LANES), BF16)],
        cost_estimate=pl.CostEstimate(
            flops=len(acts) * 4 * count * half * LANES,
            bytes_accessed=len(acts) * 2 * count * half,
            transcendentals=0,
        ),
        compiler_params=params(24),
    )(*acts, mixed)


def per_device(hidden, codes, scales, sign_bits):
    row_count, local_width = hidden.shape
    x_count, y_count = lax.axis_size("x"), lax.axis_size("y")
    tp_count = lax.axis_size("z") * lax.axis_size("core")
    rows = local_width // PARTS // y_count
    padded = -(-2 * rows // (STEP * tp_count)) * STEP * tp_count

    weight = weight_share(codes, scales, rows, padded)
    pieces = weight.reshape(tp_count, padded // tp_count, LANES)
    pieces = lax.all_to_all(pieces, ("z", "core"), 0, 0, tiled=True)

    same, other = turn(hidden, sign_bits)
    pieces, same, other = lax.optimization_barrier((pieces, same, other))
    acts = [same]
    for flip in range(1, x_count):
        route = [(x, x ^ flip) for x in range(x_count)]
        acts.append(lax.ppermute(same if flip < SIDES else other, "x", route))

    mixed = mix(pieces.reshape(padded, LANES), tp_count, y_count)
    mixed = mixed.reshape(y_count * tp_count, padded // tp_count, LANES)
    mixed = lax.all_to_all(mixed, ("y", "z", "core"), 0, 0, tiled=True)

    part_sum = project(acts, mixed.reshape(y_count, padded, LANES), rows)
    out_rows = row_count // tp_count
    parts = lax.all_to_all(
        part_sum.reshape(x_count * tp_count, out_rows, 2 * LANES), ("x", "z", "core"), 0, 0, tiled=True
    )
    parts = parts.reshape(PARTS, SIDES, tp_count, out_rows, 2 * LANES).astype(F32)
    total = jnp.sum(parts, axis=(0, 2))
    return jnp.concatenate([total[side] for side in range(SIDES)], axis=-1).astype(BF16)


def solution(mesh):
    devices = mesh.devices.reshape(4, 8, 8, 2)
    grid = Mesh(devices, ("x", "y", "z", "core"))
    rep, tp = ("x", "y"), ("z", "core")
    return jax.shard_map(
        per_device,
        mesh=grid,
        in_specs=(P(rep, tp), P(tp, None), P(tp, None), P(tp)),
        out_specs=P(rep + tp, None),
        check_vma=False,
    )
```

```python
import jax
import jax.numpy as jnp
from jax import lax
from jax.experimental import pallas as pl
from jax.experimental.pallas import tpu as pltpu
from jax.sharding import Mesh, PartitionSpec as P

BF16 = jnp.bfloat16
F32 = jnp.float32
TURN = 256
GROUP = 128
LANES = 128
STEP = 16
PARTS, SIDES = 2, 2


def sylvester(matrix_size):
    indices = jnp.arange(matrix_size, dtype=jnp.int32)
    common = jnp.bitwise_and(indices[:, None], indices[None, :])
    parity = jnp.zeros((matrix_size, matrix_size), jnp.int32)
    for place in range(matrix_size.bit_length() - 1):
        parity = parity + jnp.bitwise_and(jnp.right_shift(common, place), 1)
    return 1.0 - 2.0 * jnp.bitwise_and(parity, 1).astype(F32)


def params(mib):
    return pltpu.CompilerParams(vmem_limit_bytes=mib * 1024 * 1024)


def weight_kernel(rows, padded, codes_ref, scales_ref, out_ref, code_vmem, sem):
    x, y = lax.axis_index("x"), lax.axis_index("y")
    share = (x // SIDES) * lax.axis_size("y") + y
    low = pl.multiple_of((x % SIDES) * (2 * LANES), 2 * LANES)
    copy = pltpu.make_async_copy(
        codes_ref.at[pl.ds(pl.multiple_of(share * rows, STEP), rows), pl.ds(low, 2 * LANES)],
        code_vmem,
        sem,
    )
    copy.start()
    out_ref[2 * rows :] = jnp.zeros((padded - 2 * rows, LANES), BF16)
    copy.wait()
    for step in range(rows // STEP):
        group = (share * (rows // STEP) + step) // (GROUP // STEP)
        scale = scales_ref[pl.ds(group, 1), pl.ds(low, 2 * LANES)]
        value = code_vmem[step * STEP : (step + 1) * STEP].astype(F32) * scale
        value = value.astype(BF16)
        for side in range(2):
            at = side * rows + step * STEP
            out_ref[at : at + STEP] = value[:, side * LANES : (side + 1) * LANES]


def weight_share(codes, scales, rows, padded):
    return pl.pallas_call(
        lambda *refs: weight_kernel(rows, padded, *refs),
        out_shape=jax.ShapeDtypeStruct((padded, LANES), BF16),
        in_specs=[
            pl.BlockSpec(memory_space=pl.ANY),
            pl.BlockSpec(memory_space=pltpu.VMEM),
        ],
        scratch_shapes=[pltpu.VMEM((rows, 2 * LANES), BF16), pltpu.SemaphoreType.DMA],
        cost_estimate=pl.CostEstimate(
            flops=2 * rows * LANES, bytes_accessed=8 * rows * LANES, transcendentals=0
        ),
        compiler_params=params(56),
    )(codes, scales)


def mix_kernel(count, in_ref, out_ref):
    rows = in_ref.shape[0] // count
    for low in range(0, rows, STEP):
        blocks = [
            in_ref[p * rows + low : p * rows + low + STEP].astype(F32) for p in range(count)
        ]
        stride = 1
        while stride < count:
            for p in range(count):
                if not p & stride:
                    a, b = blocks[p], blocks[p + stride]
                    blocks[p], blocks[p + stride] = a + b, a - b
            stride *= 2
        for q in range(count):
            value = (blocks[q] * (count**-0.5)).astype(BF16)
            for y in range(out_ref.shape[0]):
                out_ref[y, q, low : low + STEP] = value


def mix(parts, tp_count, y_count):
    rows = parts.shape[0] // tp_count
    return pl.pallas_call(
        lambda *refs: mix_kernel(tp_count, *refs),
        out_shape=jax.ShapeDtypeStruct((y_count, tp_count, rows, LANES), BF16),
        cost_estimate=pl.CostEstimate(
            flops=8 * parts.size, bytes_accessed=20 * parts.size, transcendentals=0
        ),
        compiler_params=params(24),
    )(parts)


def turn_kernel(hidden_ref, bits_ref, table_ref, same_ref, other_ref):
    rows, width = hidden_ref.shape
    half = width // PARTS
    own = lax.axis_index("x") // SIDES
    table = table_ref[...]
    for keep in range(PARTS):

        @pl.when(own == keep)
        def _(keep=keep):
            for low in range(0, width, TURN):
                hidden = hidden_ref[:, low : low + TURN]
                plus = bits_ref[:, low : low + TURN] == 1
                signed = hidden * jnp.where(plus, 1.0, -1.0).astype(BF16)
                turned = jnp.dot(signed, table, preferred_element_type=F32).astype(BF16)
                for piece in range(0, TURN, LANES):
                    part, inside = divmod(low + piece, half)
                    out_ref = same_ref if part == keep else other_ref
                    out_ref[:, inside : inside + LANES] = turned[:, piece : piece + LANES]


def turn(hidden, sign_bits):
    rows, width = hidden.shape
    table = (sylvester(TURN) * (1.0 / 16.0)).astype(BF16)
    half = jax.ShapeDtypeStruct((rows, width // PARTS), BF16)
    return pl.pallas_call(
        turn_kernel,
        out_shape=(half, half),
        cost_estimate=pl.CostEstimate(
            flops=2 * rows * width * TURN, bytes_accessed=4 * rows * width, transcendentals=0
        ),
        compiler_params=params(24),
    )(hidden, sign_bits.reshape(1, width), table)


def project_kernel(rows, act0, act1, act2, act3, mixed_ref, out_ref, weight_vmem):
    for y in range(mixed_ref.shape[0]):
        for side in range(2):
            weight_vmem[y * rows : (y + 1) * rows, side * LANES : (side + 1) * LANES] = mixed_ref[
                y, side * rows : (side + 1) * rows
            ]
    x = lax.axis_index("x")
    for flip, act_ref in enumerate((act0, act1, act2, act3)):
        value = jnp.dot(act_ref[...], weight_vmem[...], preferred_element_type=F32)
        out_ref[jnp.bitwise_xor(x, flip)] = value.astype(BF16)


def project(acts, mixed, rows):
    count, half = acts[0].shape
    return pl.pallas_call(
        lambda *refs: project_kernel(rows, *refs),
        out_shape=jax.ShapeDtypeStruct((len(acts), count, 2 * LANES), BF16),
        scratch_shapes=[pltpu.VMEM((half, 2 * LANES), BF16)],
        cost_estimate=pl.CostEstimate(
            flops=len(acts) * 4 * count * half * LANES,
            bytes_accessed=len(acts) * 2 * count * half,
            transcendentals=0,
        ),
        compiler_params=params(24),
    )(*acts, mixed)


def per_device(hidden, codes, scales, sign_bits):
    row_count, local_width = hidden.shape
    x_count, y_count = lax.axis_size("x"), lax.axis_size("y")
    tp_count = lax.axis_size("z") * lax.axis_size("core")
    rows = local_width // PARTS // y_count
    padded = -(-2 * rows // (STEP * tp_count)) * STEP * tp_count

    weight = weight_share(codes, scales, rows, padded)
    pieces = weight.reshape(tp_count, padded // tp_count, LANES)
    pieces = lax.all_to_all(pieces, ("z", "core"), 0, 0, tiled=True)

    same, other = turn(hidden, sign_bits)
    pieces = lax.optimization_barrier((pieces, same, other))[0]
    acts = [same]
    for flip in range(1, x_count):
        route = [(x, x ^ flip) for x in range(x_count)]
        acts.append(lax.ppermute(same if flip < SIDES else other, "x", route))

    mixed = mix(pieces.reshape(padded, LANES), tp_count, 1)
    mixed = lax.all_to_all(mixed[0], ("z", "core"), 0, 0, tiled=True)
    mixed = lax.all_gather(mixed.reshape(padded, LANES)[: 2 * rows], "y")

    part_sum = project(acts, mixed, rows)
    out_rows = row_count // tp_count
    parts = lax.all_to_all(
        part_sum.reshape(x_count * tp_count, out_rows, 2 * LANES), ("x", "z", "core"), 0, 0, tiled=True
    )
    parts = parts.reshape(PARTS, SIDES, tp_count, out_rows, 2 * LANES).astype(F32)
    total = jnp.sum(parts, axis=(0, 2))
    return jnp.concatenate([total[side] for side in range(SIDES)], axis=-1).astype(BF16)


def solution(mesh):
    devices = mesh.devices.reshape(4, 8, 8, 2)
    grid = Mesh(devices, ("x", "y", "z", "core"))
    rep, tp = ("x", "y"), ("z", "core")
    return jax.shard_map(
        per_device,
        mesh=grid,
        in_specs=(P(rep, tp), P(tp, None), P(tp, None), P(tp)),
        out_specs=P(rep + tp, None),
        check_vma=False,
    )
```

```python
import jax
import jax.numpy as jnp
from jax import lax
from jax.experimental import pallas as pl
from jax.experimental.pallas import tpu as pltpu
from jax.sharding import Mesh, PartitionSpec as P

BF16 = jnp.bfloat16
F32 = jnp.float32
TURN = 256
GROUP = 128
LANES = 128
STEP = 16
PARTS, SIDES = 2, 2


def sylvester(matrix_size):
    indices = jnp.arange(matrix_size, dtype=jnp.int32)
    common = jnp.bitwise_and(indices[:, None], indices[None, :])
    parity = jnp.zeros((matrix_size, matrix_size), jnp.int32)
    for place in range(matrix_size.bit_length() - 1):
        parity = parity + jnp.bitwise_and(jnp.right_shift(common, place), 1)
    return 1.0 - 2.0 * jnp.bitwise_and(parity, 1).astype(F32)


def params(mib):
    return pltpu.CompilerParams(vmem_limit_bytes=mib * 1024 * 1024)


def weight_kernel(rows, padded, codes_ref, scales_ref, out_ref, code_vmem, scale_vmem, sem):
    x, y = lax.axis_index("x"), lax.axis_index("y")
    share = (x // SIDES) * lax.axis_size("y") + y
    low = pl.multiple_of((x % SIDES) * (2 * LANES), 2 * LANES)
    columns = pl.ds(low, 2 * LANES)
    code_rows = pl.ds(pl.multiple_of(share * rows, STEP), rows)
    code_copy = pltpu.make_async_copy(codes_ref.at[code_rows, columns], code_vmem, sem.at[0])
    scale_copy = pltpu.make_async_copy(scales_ref.at[:, columns], scale_vmem, sem.at[1])
    code_copy.start()
    scale_copy.start()
    out_ref[2 * rows :] = jnp.zeros((padded - 2 * rows, LANES), BF16)
    code_copy.wait()
    scale_copy.wait()
    for step in range(rows // STEP):
        group = (share * (rows // STEP) + step) // (GROUP // STEP)
        scale = scale_vmem[pl.ds(group, 1)]
        value = code_vmem[step * STEP : (step + 1) * STEP].astype(F32) * scale
        value = value.astype(BF16)
        for side in range(2):
            at = side * rows + step * STEP
            out_ref[at : at + STEP] = value[:, side * LANES : (side + 1) * LANES]


def weight_share(codes, scales, rows, padded):
    return pl.pallas_call(
        lambda *refs: weight_kernel(rows, padded, *refs),
        out_shape=jax.ShapeDtypeStruct((padded, LANES), BF16),
        in_specs=[pl.BlockSpec(memory_space=pl.ANY)] * 2,
        scratch_shapes=[
            pltpu.VMEM((rows, 2 * LANES), BF16),
            pltpu.VMEM((scales.shape[0], 2 * LANES), F32),
            pltpu.SemaphoreType.DMA((2,)),
        ],
        cost_estimate=pl.CostEstimate(
            flops=2 * rows * LANES, bytes_accessed=8 * rows * LANES, transcendentals=0
        ),
        compiler_params=params(56),
    )(codes, scales)


def mix_kernel(count, in_ref, out_ref):
    rows = in_ref.shape[0] // count
    for low in range(0, rows, STEP):
        blocks = [
            in_ref[p * rows + low : p * rows + low + STEP].astype(F32) for p in range(count)
        ]
        stride = 1
        while stride < count:
            for p in range(count):
                if not p & stride:
                    a, b = blocks[p], blocks[p + stride]
                    blocks[p], blocks[p + stride] = a + b, a - b
            stride *= 2
        for q in range(count):
            value = (blocks[q] * (count**-0.5)).astype(BF16)
            for y in range(out_ref.shape[0]):
                out_ref[y, q, low : low + STEP] = value


def mix(parts, tp_count, y_count):
    rows = parts.shape[0] // tp_count
    return pl.pallas_call(
        lambda *refs: mix_kernel(tp_count, *refs),
        out_shape=jax.ShapeDtypeStruct((y_count, tp_count, rows, LANES), BF16),
        cost_estimate=pl.CostEstimate(
            flops=8 * parts.size, bytes_accessed=20 * parts.size, transcendentals=0
        ),
        compiler_params=params(24),
    )(parts)


def turn_kernel(wanted, hidden_ref, bits_ref, table_ref, *out_refs):
    rows, width = hidden_ref.shape
    half = width // PARTS
    cores = lax.axis_size("core")
    chips = lax.axis_size("z")
    run = rows // (chips * cores)
    own = lax.axis_index("x") // SIDES
    table = table_ref[...]
    for keep in range(PARTS):

        @pl.when(own == keep)
        def _(keep=keep):
            for low in range(0, width, TURN):
                spots = [divmod(at, half) for at in range(low, low + TURN, LANES)]
                if not any((part != keep) in wanted for part, _ in spots):
                    continue
                hidden = hidden_ref[:, low : low + TURN]
                plus = bits_ref[:, low : low + TURN] == 1
                signed = hidden * jnp.where(plus, 1.0, -1.0).astype(BF16)
                turned = jnp.dot(signed, table, preferred_element_type=F32).astype(BF16)
                for piece, (part, inside) in enumerate(spots):
                    if (part != keep) not in wanted:
                        continue
                    out_ref = out_refs[wanted.index(part != keep)]
                    value = turned[:, piece * LANES : (piece + 1) * LANES]
                    for chip in range(chips):
                        for core in range(cores):
                            source = (chip * cores + core) * run
                            target = (core * chips + chip) * run
                            out_ref[target : target + run, inside : inside + LANES] = value[
                                source : source + run
                            ]


def turn(hidden, sign_bits, wanted):
    rows, width = hidden.shape
    table = (sylvester(TURN) * (1.0 / 16.0)).astype(BF16)
    half = jax.ShapeDtypeStruct((rows, width // PARTS), BF16)
    return pl.pallas_call(
        lambda *refs: turn_kernel(wanted, *refs),
        out_shape=[half for _ in wanted],
        cost_estimate=pl.CostEstimate(
            flops=2 * rows * width * TURN, bytes_accessed=4 * rows * width, transcendentals=0
        ),
        compiler_params=params(24),
    )(hidden, sign_bits.reshape(1, width), table)


def project_kernel(rows, give, act0, act1, act2, act3, mixed_ref, out_ref, weight_vmem):
    for y in range(mixed_ref.shape[0]):
        for side in range(2):
            weight_vmem[y * rows : (y + 1) * rows, side * LANES : (side + 1) * LANES] = mixed_ref[
                y, side * rows : (side + 1) * rows
            ]
    x, core = lax.axis_index("x"), lax.axis_index("core")
    count = out_ref.shape[1]
    spot = pl.ds(pl.multiple_of(jnp.bitwise_xor(core, give) * count, count), count)
    for flip, act_ref in enumerate((act0, act1, act2, act3)):
        value = jnp.dot(act_ref[spot], weight_vmem[...], preferred_element_type=F32)
        out_ref[jnp.bitwise_xor(x, flip)] = value.astype(out_ref.dtype)


def project(acts, mixed, rows, give):
    count, half = acts[0].shape
    return pl.pallas_call(
        lambda *refs: project_kernel(rows, give, *refs),
        out_shape=jax.ShapeDtypeStruct(
            (len(acts), count // 2, 2 * LANES), BF16 if give else F32
        ),
        scratch_shapes=[pltpu.VMEM((half, 2 * LANES), BF16)],
        cost_estimate=pl.CostEstimate(
            flops=len(acts) * 2 * count * half * LANES,
            bytes_accessed=len(acts) * count * half,
            transcendentals=0,
        ),
        compiler_params=params(24),
    )(*acts, mixed)


def swap(block, flip):
    return lax.ppermute(block, "x", [(x, x ^ flip) for x in range(lax.axis_size("x"))])


def per_device(hidden, codes, scales, sign_bits):
    row_count, local_width = hidden.shape
    x_count, y_count = lax.axis_size("x"), lax.axis_size("y")
    tp_count = lax.axis_size("z") * lax.axis_size("core")
    rows = local_width // PARTS // y_count
    padded = -(-2 * rows // (STEP * tp_count)) * STEP * tp_count

    weight = weight_share(codes, scales, rows, padded)
    pieces = weight.reshape(tp_count, padded // tp_count, LANES)
    pieces = lax.all_to_all(pieces, ("z", "core"), 0, 0, tiled=True)

    same, other = turn(hidden, sign_bits, [0, 1])
    pieces = lax.optimization_barrier((pieces, same, other))[0]
    beside, across, corner = swap(same, 1), swap(other, SIDES), swap(other, SIDES + 1)

    mixed = mix(pieces.reshape(padded, LANES), tp_count, 1)
    mixed = lax.all_to_all(mixed[0], ("z", "core"), 0, 0, tiled=True)
    mixed = lax.all_gather(mixed.reshape(padded, LANES)[: 2 * rows], "y")

    acts = [same, beside, across, corner]
    give = project(acts, mixed, rows, 1)
    got = lax.ppermute(give, "core", [(0, 1), (1, 0)])
    chip_sum = (project(acts, mixed, rows, 0) + got.astype(F32)).astype(BF16)
    out_rows = row_count // tp_count
    blocks = x_count * lax.axis_size("z")
    parts = chip_sum.reshape(blocks, out_rows, 2 * LANES)
    parts = lax.all_to_all(parts, ("x", "z"), 0, 0, tiled=True)
    parts = parts.reshape(PARTS, SIDES, -1, out_rows, 2 * LANES).astype(F32)
    total = jnp.sum(parts, axis=(0, 2))
    return jnp.concatenate([total[side] for side in range(SIDES)], axis=-1).astype(BF16)


def solution(mesh):
    devices = mesh.devices.reshape(4, 8, 8, 2)
    grid = Mesh(devices, ("x", "y", "z", "core"))
    rep, tp = ("x", "y"), ("z", "core")
    return jax.shard_map(
        per_device,
        mesh=grid,
        in_specs=(P(rep, tp), P(tp, None), P(tp, None), P(tp)),
        out_specs=P(rep + tp, None),
        check_vma=False,
    )
```

```python
import jax
import jax.numpy as jnp
from jax import lax
from jax.experimental import pallas as pl
from jax.experimental.pallas import tpu as pltpu
from jax.sharding import Mesh, PartitionSpec as P

BF16 = jnp.bfloat16
F32 = jnp.float32
TURN = 256
GROUP = 128
LANES = 128
STEP = 16
CORES = 2
PARTS, SIDES = 2, 2


def sylvester(matrix_size):
    indices = jnp.arange(matrix_size, dtype=jnp.int32)
    common = jnp.bitwise_and(indices[:, None], indices[None, :])
    parity = jnp.zeros((matrix_size, matrix_size), jnp.int32)
    for place in range(matrix_size.bit_length() - 1):
        parity = parity + jnp.bitwise_and(jnp.right_shift(common, place), 1)
    return 1.0 - 2.0 * jnp.bitwise_and(parity, 1).astype(F32)


def params(mib):
    return pltpu.CompilerParams(vmem_limit_bytes=mib * 1024 * 1024)


def weight_kernel(rows, padded, codes_ref, scales_ref, out_ref, code_vmem, scale_vmem, sem):
    x, far, near = (lax.axis_index(name) for name in ("x", "far", "near"))
    share = ((x // SIDES) * lax.axis_size("far") + far) * lax.axis_size("near") + near
    low = pl.multiple_of((x % SIDES) * (2 * LANES), 2 * LANES)
    columns = pl.ds(low, 2 * LANES)
    code_rows = pl.ds(pl.multiple_of(share * rows, STEP), rows)
    code_copy = pltpu.make_async_copy(codes_ref.at[code_rows, columns], code_vmem, sem.at[0])
    scale_copy = pltpu.make_async_copy(scales_ref.at[:, columns], scale_vmem, sem.at[1])
    code_copy.start()
    scale_copy.start()
    out_ref[2 * rows :] = jnp.zeros((padded - 2 * rows, LANES), BF16)
    code_copy.wait()
    scale_copy.wait()
    for step in range(rows // STEP):
        group = (share * (rows // STEP) + step) // (GROUP // STEP)
        scale = scale_vmem[pl.ds(group, 1)]
        value = code_vmem[step * STEP : (step + 1) * STEP].astype(F32) * scale
        value = value.astype(BF16)
        for side in range(2):
            at = side * rows + step * STEP
            out_ref[at : at + STEP] = value[:, side * LANES : (side + 1) * LANES]


def weight_share(codes, scales, rows, padded):
    return pl.pallas_call(
        lambda *refs: weight_kernel(rows, padded, *refs),
        out_shape=jax.ShapeDtypeStruct((padded, LANES), BF16),
        in_specs=[pl.BlockSpec(memory_space=pl.ANY)] * 2,
        scratch_shapes=[
            pltpu.VMEM((rows, 2 * LANES), BF16),
            pltpu.VMEM((scales.shape[0], 2 * LANES), F32),
            pltpu.SemaphoreType.DMA((2,)),
        ],
        cost_estimate=pl.CostEstimate(
            flops=2 * rows * LANES, bytes_accessed=8 * rows * LANES, transcendentals=0
        ),
        compiler_params=params(56),
    )(codes, scales)


def mix_kernel(count, in_ref, out_ref):
    rows = in_ref.shape[0] // count
    for low in range(0, rows, STEP):
        blocks = [
            in_ref[p * rows + low : p * rows + low + STEP].astype(F32) for p in range(count)
        ]
        stride = 1
        while stride < count:
            for p in range(count):
                if not p & stride:
                    a, b = blocks[p], blocks[p + stride]
                    blocks[p], blocks[p + stride] = a + b, a - b
            stride *= 2
        for q in range(count):
            value = (blocks[q] * (count**-0.5)).astype(BF16)
            for y in range(out_ref.shape[0]):
                out_ref[y, q, low : low + STEP] = value


def mix(parts, tp_count, copies):
    rows = parts.shape[0] // tp_count
    return pl.pallas_call(
        lambda *refs: mix_kernel(tp_count, *refs),
        out_shape=jax.ShapeDtypeStruct((copies, tp_count, rows, LANES), BF16),
        cost_estimate=pl.CostEstimate(
            flops=8 * parts.size, bytes_accessed=20 * parts.size, transcendentals=0
        ),
        compiler_params=params(24),
    )(parts)


def turn_kernel(hidden_ref, bits_ref, table_ref, *out_refs):
    same_refs, other_ref = out_refs[:CORES], out_refs[CORES]
    rows, width = hidden_ref.shape
    half = width // PARTS
    chips = lax.axis_size("z")
    run = rows // (chips * CORES)
    own = lax.axis_index("x") // SIDES
    table = table_ref[...]
    for keep in range(PARTS):

        @pl.when(own == keep)
        def _(keep=keep):
            for low in range(0, width, TURN):
                plus = bits_ref[:, low : low + TURN] == 1
                sign = jnp.where(plus, 1.0, -1.0).astype(BF16)
                for core in range(CORES):
                    runs = [(chip * CORES + core) * run for chip in range(chips)]
                    hidden = [hidden_ref[at : at + run, low : low + TURN] for at in runs]
                    signed = jnp.concatenate(hidden) * sign
                    turned = jnp.dot(signed, table, preferred_element_type=F32).astype(BF16)
                    for piece in range(0, TURN, LANES):
                        part, inside = divmod(low + piece, half)
                        lanes = slice(inside, inside + LANES)
                        value = turned[:, piece : piece + LANES]
                        if part == keep:
                            same_refs[core][:, lanes] = value
                        else:
                            at = core * chips * run
                            other_ref[at : at + chips * run, lanes] = value


def turn(hidden, sign_bits):
    rows, width = hidden.shape
    table = (sylvester(TURN) * (1.0 / 16.0)).astype(BF16)
    whole = jax.ShapeDtypeStruct((rows, width // PARTS), BF16)
    block = jax.ShapeDtypeStruct((rows // CORES, width // PARTS), BF16)
    return pl.pallas_call(
        turn_kernel,
        out_shape=[block, block, whole],
        cost_estimate=pl.CostEstimate(
            flops=2 * rows * width * TURN, bytes_accessed=4 * rows * width, transcendentals=0
        ),
        compiler_params=params(24),
    )(hidden, sign_bits.reshape(1, width), table)


def project_kernel(rows, give, *refs):
    (*act_refs, mixed_ref, out_ref, weight_vmem) = refs
    for y in range(mixed_ref.shape[0]):
        for side in range(2):
            weight_vmem[y * rows : (y + 1) * rows, side * LANES : (side + 1) * LANES] = mixed_ref[
                y, side * rows : (side + 1) * rows
            ]
    same, beside, across, corner = act_refs[0:2], act_refs[2:4], act_refs[4], act_refs[5]
    x, core = lax.axis_index("x"), lax.axis_index("core")
    count = out_ref.shape[1]
    for half in range(CORES):

        @pl.when(jnp.bitwise_xor(core, give) == half)
        def _(half=half):
            at = slice(half * count, (half + 1) * count)
            acts = same[half][...], beside[half][...], across[at], corner[at]
            for flip, act in enumerate(acts):
                value = jnp.dot(act, weight_vmem[...], preferred_element_type=F32)
                out_ref[jnp.bitwise_xor(x, flip)] = value.astype(out_ref.dtype)


def project(acts, mixed, rows, give):
    count, half = acts[0].shape
    groups = PARTS * SIDES
    return pl.pallas_call(
        lambda *refs: project_kernel(rows, give, *refs),
        out_shape=jax.ShapeDtypeStruct((groups, count, 2 * LANES), BF16 if give else F32),
        scratch_shapes=[pltpu.VMEM((half, 2 * LANES), BF16)],
        cost_estimate=pl.CostEstimate(
            flops=groups * 4 * count * half * LANES,
            bytes_accessed=groups * 2 * count * half,
            transcendentals=0,
        ),
        compiler_params=params(24),
    )(*acts, mixed)


def total_kernel(parts_ref, out_ref):
    parts, sides, chips, _, width = parts_ref.shape
    for side in range(sides):
        total = None
        for part in range(parts):
            for chip in range(chips):
                value = parts_ref[part, side, chip].astype(F32)
                total = value if total is None else total + value
        out_ref[:, side * width : (side + 1) * width] = total.astype(BF16)


def total(parts):
    _, sides, _, rows, width = parts.shape
    return pl.pallas_call(
        total_kernel,
        out_shape=jax.ShapeDtypeStruct((rows, sides * width), BF16),
        cost_estimate=pl.CostEstimate(
            flops=parts.size, bytes_accessed=2 * parts.size, transcendentals=0
        ),
        compiler_params=params(24),
    )(parts)


def swap(block, flip):
    return lax.ppermute(block, "x", [(x, x ^ flip) for x in range(lax.axis_size("x"))])


def per_device(hidden, codes, scales, sign_bits):
    row_count, local_width = hidden.shape
    x_count, far_count = lax.axis_size("x"), lax.axis_size("far")
    tp_count = lax.axis_size("z") * lax.axis_size("core")
    rows = local_width // PARTS // (far_count * lax.axis_size("near"))
    padded = -(-2 * rows // (STEP * tp_count)) * STEP * tp_count

    weight = weight_share(codes, scales, rows, padded)
    pieces = weight.reshape(tp_count, padded // tp_count, LANES)
    pieces = lax.all_to_all(pieces, ("z", "core"), 0, 0, tiled=True)

    same0, same1, other = turn(hidden, sign_bits)
    pieces = lax.optimization_barrier((pieces, other))[0]
    across, corner = swap(other, SIDES), swap(other, SIDES + 1)
    beside = swap(same0, 1), swap(same1, 1)

    near_count = lax.axis_size("near")
    mixed = mix(pieces.reshape(padded, LANES), tp_count, near_count)
    mixed = mixed.reshape(near_count * tp_count, padded // tp_count, LANES)
    mixed = lax.all_to_all(mixed, ("near", "z", "core"), 0, 0, tiled=True)
    mixed = mixed.reshape(near_count, padded, LANES)[:, : 2 * rows]
    mixed = lax.all_gather(mixed, "far", tiled=True)

    acts = [same0, same1, *beside, across, corner]
    give = project(acts, mixed, rows, 1)
    got = lax.ppermute(give, "core", [(0, 1), (1, 0)])
    chip_sum = (project(acts, mixed, rows, 0) + got.astype(F32)).astype(BF16)
    out_rows = row_count // tp_count
    blocks = x_count * lax.axis_size("z")
    parts = chip_sum.reshape(blocks, out_rows, 2 * LANES)
    parts = lax.all_to_all(parts, ("x", "z"), 0, 0, tiled=True)
    return total(parts.reshape(PARTS, SIDES, -1, out_rows, 2 * LANES))


def solution(mesh):
    devices = mesh.devices.reshape(4, 4, 2, 8, 2)
    grid = Mesh(devices, ("x", "far", "near", "z", "core"))
    rep, tp = ("x", "far", "near"), ("z", "core")
    return jax.shard_map(
        per_device,
        mesh=grid,
        in_specs=(P(rep, tp), P(tp, None), P(tp, None), P(tp)),
        out_specs=P(rep + tp, None),
        check_vma=False,
    )
```

```python
import jax
import jax.numpy as jnp
from jax import lax
from jax.experimental import pallas as pl
from jax.experimental.pallas import tpu as pltpu
from jax.sharding import Mesh, PartitionSpec as P

BF16 = jnp.bfloat16
F32 = jnp.float32
TURN = 256
GROUP = 128
LANES = 128
STEP = 16
CORES = 2
PARTS, SIDES = 2, 2


def sylvester(matrix_size):
    indices = jnp.arange(matrix_size, dtype=jnp.int32)
    common = jnp.bitwise_and(indices[:, None], indices[None, :])
    parity = jnp.zeros((matrix_size, matrix_size), jnp.int32)
    for place in range(matrix_size.bit_length() - 1):
        parity = parity + jnp.bitwise_and(jnp.right_shift(common, place), 1)
    return 1.0 - 2.0 * jnp.bitwise_and(parity, 1).astype(F32)


def params(mib):
    return pltpu.CompilerParams(vmem_limit_bytes=mib * 1024 * 1024)


def weight_kernel(rows, padded, codes_ref, scales_ref, out_ref, code_vmem, scale_vmem, sem):
    x, far, near = (lax.axis_index(name) for name in ("x", "far", "near"))
    share = ((x % PARTS) * lax.axis_size("far") + far) * lax.axis_size("near") + near
    low = pl.multiple_of((x // PARTS) * (2 * LANES), 2 * LANES)
    columns = pl.ds(low, 2 * LANES)
    code_rows = pl.ds(pl.multiple_of(share * rows, STEP), rows)
    code_copy = pltpu.make_async_copy(codes_ref.at[code_rows, columns], code_vmem, sem.at[0])
    scale_copy = pltpu.make_async_copy(scales_ref.at[:, columns], scale_vmem, sem.at[1])
    code_copy.start()
    scale_copy.start()
    out_ref[2 * rows :] = jnp.zeros((padded - 2 * rows, LANES), BF16)
    code_copy.wait()
    scale_copy.wait()
    for step in range(rows // STEP):
        group = (share * (rows // STEP) + step) // (GROUP // STEP)
        scale = scale_vmem[pl.ds(group, 1)]
        value = code_vmem[step * STEP : (step + 1) * STEP].astype(F32) * scale
        value = value.astype(BF16)
        for side in range(2):
            at = side * rows + step * STEP
            out_ref[at : at + STEP] = value[:, side * LANES : (side + 1) * LANES]


def weight_share(codes, scales, rows, padded):
    return pl.pallas_call(
        lambda *refs: weight_kernel(rows, padded, *refs),
        out_shape=jax.ShapeDtypeStruct((padded, LANES), BF16),
        in_specs=[pl.BlockSpec(memory_space=pl.ANY)] * 2,
        scratch_shapes=[
            pltpu.VMEM((rows, 2 * LANES), BF16),
            pltpu.VMEM((scales.shape[0], 2 * LANES), F32),
            pltpu.SemaphoreType.DMA((2,)),
        ],
        cost_estimate=pl.CostEstimate(
            flops=2 * rows * LANES, bytes_accessed=8 * rows * LANES, transcendentals=0
        ),
        compiler_params=params(56),
    )(codes, scales)


def mix_kernel(count, in_ref, out_ref):
    rows = in_ref.shape[0] // count
    for low in range(0, rows, STEP):
        blocks = [
            in_ref[p * rows + low : p * rows + low + STEP].astype(F32) for p in range(count)
        ]
        stride = 1
        while stride < count:
            for p in range(count):
                if not p & stride:
                    a, b = blocks[p], blocks[p + stride]
                    blocks[p], blocks[p + stride] = a + b, a - b
            stride *= 2
        for q in range(count):
            value = (blocks[q] * (count**-0.5)).astype(BF16)
            for y in range(out_ref.shape[0]):
                out_ref[y, q, low : low + STEP] = value


def mix(parts, tp_count, copies):
    rows = parts.shape[0] // tp_count
    return pl.pallas_call(
        lambda *refs: mix_kernel(tp_count, *refs),
        out_shape=jax.ShapeDtypeStruct((copies, tp_count, rows, LANES), BF16),
        cost_estimate=pl.CostEstimate(
            flops=8 * parts.size, bytes_accessed=20 * parts.size, transcendentals=0
        ),
        compiler_params=params(24),
    )(parts)


def turn_kernel(hidden_ref, bits_ref, table_ref, *out_refs):
    same_refs, other_ref = out_refs[:CORES], out_refs[CORES]
    rows, width = hidden_ref.shape
    half = width // PARTS
    chips = lax.axis_size("z")
    run = rows // (chips * CORES)
    own = lax.axis_index("x") % PARTS
    table = table_ref[...]
    for keep in range(PARTS):

        @pl.when(own == keep)
        def _(keep=keep):
            for low in range(0, width, TURN):
                plus = bits_ref[:, low : low + TURN] == 1
                sign = jnp.where(plus, 1.0, -1.0).astype(BF16)
                for core in range(CORES):
                    runs = [(chip * CORES + core) * run for chip in range(chips)]
                    hidden = [hidden_ref[at : at + run, low : low + TURN] for at in runs]
                    signed = jnp.concatenate(hidden) * sign
                    turned = jnp.dot(signed, table, preferred_element_type=F32).astype(BF16)
                    for piece in range(0, TURN, LANES):
                        part, inside = divmod(low + piece, half)
                        lanes = slice(inside, inside + LANES)
                        value = turned[:, piece : piece + LANES]
                        if part == keep:
                            same_refs[core][:, lanes] = value
                        else:
                            at = core * chips * run
                            other_ref[at : at + chips * run, lanes] = value


def turn(hidden, sign_bits):
    rows, width = hidden.shape
    table = (sylvester(TURN) * (1.0 / 16.0)).astype(BF16)
    whole = jax.ShapeDtypeStruct((rows, width // PARTS), BF16)
    block = jax.ShapeDtypeStruct((rows // CORES, width // PARTS), BF16)
    return pl.pallas_call(
        turn_kernel,
        out_shape=[block, block, whole],
        cost_estimate=pl.CostEstimate(
            flops=2 * rows * width * TURN, bytes_accessed=4 * rows * width, transcendentals=0
        ),
        compiler_params=params(24),
    )(hidden, sign_bits.reshape(1, width), table)


def project_kernel(rows, give, *refs):
    (*act_refs, mixed_ref, out_ref, weight_vmem) = refs
    for y in range(mixed_ref.shape[0]):
        for side in range(2):
            weight_vmem[y * rows : (y + 1) * rows, side * LANES : (side + 1) * LANES] = mixed_ref[
                y, side * rows : (side + 1) * rows
            ]
    same, beside, across, corner = act_refs[0:2], act_refs[2], act_refs[3:5], act_refs[5]
    x, core = lax.axis_index("x"), lax.axis_index("core")
    count = out_ref.shape[1]
    for half in range(CORES):

        @pl.when(jnp.bitwise_xor(core, give) == half)
        def _(half=half):
            at = slice(half * count, (half + 1) * count)
            acts = same[half][...], beside[at], across[half][...], corner[at]
            for flip, act in enumerate(acts):
                value = jnp.dot(act, weight_vmem[...], preferred_element_type=F32)
                out_ref[jnp.bitwise_xor(x, flip)] = value.astype(out_ref.dtype)


def project(acts, mixed, rows, give):
    count, half = acts[0].shape
    groups = PARTS * SIDES
    return pl.pallas_call(
        lambda *refs: project_kernel(rows, give, *refs),
        out_shape=jax.ShapeDtypeStruct((groups, count, 2 * LANES), BF16 if give else F32),
        scratch_shapes=[pltpu.VMEM((half, 2 * LANES), BF16)],
        cost_estimate=pl.CostEstimate(
            flops=groups * 4 * count * half * LANES,
            bytes_accessed=groups * 2 * count * half,
            transcendentals=0,
        ),
        compiler_params=params(24),
    )(*acts, mixed)


def total_kernel(parts_ref, out_ref):
    sides, parts, chips, _, width = parts_ref.shape
    for side in range(sides):
        total = None
        for part in range(parts):
            for chip in range(chips):
                value = parts_ref[side, part, chip].astype(F32)
                total = value if total is None else total + value
        out_ref[:, side * width : (side + 1) * width] = total.astype(BF16)


def total(parts):
    sides, _, _, rows, width = parts.shape
    return pl.pallas_call(
        total_kernel,
        out_shape=jax.ShapeDtypeStruct((rows, sides * width), BF16),
        cost_estimate=pl.CostEstimate(
            flops=parts.size, bytes_accessed=2 * parts.size, transcendentals=0
        ),
        compiler_params=params(24),
    )(parts)


def swap(block, flip):
    return lax.ppermute(block, "x", [(x, x ^ flip) for x in range(lax.axis_size("x"))])


def per_device(hidden, codes, scales, sign_bits):
    row_count, local_width = hidden.shape
    x_count, far_count = lax.axis_size("x"), lax.axis_size("far")
    tp_count = lax.axis_size("z") * lax.axis_size("core")
    rows = local_width // PARTS // (far_count * lax.axis_size("near"))
    padded = -(-2 * rows // (STEP * tp_count)) * STEP * tp_count

    weight = weight_share(codes, scales, rows, padded)
    pieces = weight.reshape(tp_count, padded // tp_count, LANES)
    pieces = lax.all_to_all(pieces, ("z", "core"), 0, 0, tiled=True)

    same0, same1, other = turn(hidden, sign_bits)
    pieces = lax.optimization_barrier((pieces, other))[0]
    beside, corner = swap(other, 1), swap(other, PARTS + 1)
    across = swap(same0, PARTS), swap(same1, PARTS)

    near_count = lax.axis_size("near")
    mixed = mix(pieces.reshape(padded, LANES), tp_count, near_count)
    mixed = mixed.reshape(near_count * tp_count, padded // tp_count, LANES)
    mixed = lax.all_to_all(mixed, ("near", "z", "core"), 0, 0, tiled=True)
    mixed = mixed.reshape(near_count, padded, LANES)[:, : 2 * rows]
    mixed = lax.all_gather(mixed, "far", tiled=True)

    acts = [same0, same1, beside, *across, corner]
    give = project(acts, mixed, rows, 1)
    got = lax.ppermute(give, "core", [(0, 1), (1, 0)])
    chip_sum = (project(acts, mixed, rows, 0) + got.astype(F32)).astype(BF16)
    out_rows = row_count // tp_count
    blocks = x_count * lax.axis_size("z")
    parts = chip_sum.reshape(blocks, out_rows, 2 * LANES)
    parts = lax.all_to_all(parts, ("x", "z"), 0, 0, tiled=True)
    return total(parts.reshape(SIDES, PARTS, -1, out_rows, 2 * LANES))


def solution(mesh):
    devices = mesh.devices.reshape(4, 4, 2, 8, 2)
    grid = Mesh(devices, ("x", "far", "near", "z", "core"))
    rep, tp = ("x", "far", "near"), ("z", "core")
    return jax.shard_map(
        per_device,
        mesh=grid,
        in_specs=(P(rep, tp), P(tp, None), P(tp, None), P(tp)),
        out_specs=P(rep + tp, None),
        check_vma=False,
    )
```

```python
import jax
import jax.numpy as jnp
from jax import lax
from jax.experimental import pallas as pl
from jax.experimental.pallas import tpu as pltpu
from jax.sharding import Mesh, PartitionSpec as P

BF16 = jnp.bfloat16
F32 = jnp.float32
TURN = 256
GROUP = 128
LANES = 128
STEP = 16
CORES = 2
PARTS, SIDES = 2, 2


def sylvester(matrix_size):
    indices = jnp.arange(matrix_size, dtype=jnp.int32)
    common = jnp.bitwise_and(indices[:, None], indices[None, :])
    parity = jnp.zeros((matrix_size, matrix_size), jnp.int32)
    for place in range(matrix_size.bit_length() - 1):
        parity = parity + jnp.bitwise_and(jnp.right_shift(common, place), 1)
    return 1.0 - 2.0 * jnp.bitwise_and(parity, 1).astype(F32)


def params(mib):
    return pltpu.CompilerParams(vmem_limit_bytes=mib * 1024 * 1024)


def weight_kernel(rows, padded, codes_ref, scales_ref, out_ref, code_vmem, scale_vmem, sem):
    x, far, near = (lax.axis_index(name) for name in ("x", "far", "near"))
    share = ((x % PARTS) * lax.axis_size("far") + far) * lax.axis_size("near") + near
    low = pl.multiple_of((x // PARTS) * (2 * LANES), 2 * LANES)
    columns = pl.ds(low, 2 * LANES)
    code_rows = pl.ds(pl.multiple_of(share * rows, STEP), rows)
    code_copy = pltpu.make_async_copy(codes_ref.at[code_rows, columns], code_vmem, sem.at[0])
    scale_copy = pltpu.make_async_copy(scales_ref.at[:, columns], scale_vmem, sem.at[1])
    code_copy.start()
    scale_copy.start()
    out_ref[2 * rows :] = jnp.zeros((padded - 2 * rows, LANES), BF16)
    code_copy.wait()
    scale_copy.wait()
    for step in range(rows // STEP):
        group = (share * (rows // STEP) + step) // (GROUP // STEP)
        scale = scale_vmem[pl.ds(group, 1)]
        value = code_vmem[step * STEP : (step + 1) * STEP].astype(F32) * scale
        value = value.astype(BF16)
        for side in range(2):
            at = side * rows + step * STEP
            out_ref[at : at + STEP] = value[:, side * LANES : (side + 1) * LANES]


def weight_share(codes, scales, rows, padded):
    return pl.pallas_call(
        lambda *refs: weight_kernel(rows, padded, *refs),
        out_shape=jax.ShapeDtypeStruct((padded, LANES), BF16),
        in_specs=[pl.BlockSpec(memory_space=pl.ANY)] * 2,
        scratch_shapes=[
            pltpu.VMEM((rows, 2 * LANES), BF16),
            pltpu.VMEM((scales.shape[0], 2 * LANES), F32),
            pltpu.SemaphoreType.DMA((2,)),
        ],
        cost_estimate=pl.CostEstimate(
            flops=2 * rows * LANES, bytes_accessed=8 * rows * LANES, transcendentals=0
        ),
        compiler_params=params(56),
    )(codes, scales)


def mix_kernel(count, in_ref, out_ref):
    rows = in_ref.shape[0] // count
    for low in range(0, rows, STEP):
        blocks = [
            in_ref[p * rows + low : p * rows + low + STEP].astype(F32) for p in range(count)
        ]
        stride = 1
        while stride < count:
            for p in range(count):
                if not p & stride:
                    a, b = blocks[p], blocks[p + stride]
                    blocks[p], blocks[p + stride] = a + b, a - b
            stride *= 2
        for q in range(count):
            value = (blocks[q] * (count**-0.5)).astype(BF16)
            for y in range(out_ref.shape[0]):
                out_ref[y, q, low : low + STEP] = value


def mix(parts, tp_count, copies):
    rows = parts.shape[0] // tp_count
    return pl.pallas_call(
        lambda *refs: mix_kernel(tp_count, *refs),
        out_shape=jax.ShapeDtypeStruct((copies, tp_count, rows, LANES), BF16),
        cost_estimate=pl.CostEstimate(
            flops=8 * parts.size, bytes_accessed=20 * parts.size, transcendentals=0
        ),
        compiler_params=params(24),
    )(parts)


def turn_kernel(hidden_ref, bits_ref, table_ref, *refs):
    same_refs, (other_ref, other_vmem, sems) = refs[:CORES], refs[CORES:]
    rows, width = hidden_ref.shape
    half = width // PARTS
    chips = lax.axis_size("z")
    run = rows // (chips * CORES)
    own = lax.axis_index("x") % PARTS
    table = table_ref[...]
    for keep in range(PARTS):

        @pl.when(own == keep)
        def _(keep=keep):
            copies = []
            blocks = list(range(0, width, TURN))
            for low in blocks if keep == PARTS - 1 else blocks[::-1]:
                plus = bits_ref[:, low : low + TURN] == 1
                sign = jnp.where(plus, 1.0, -1.0).astype(BF16)
                for core in range(CORES):
                    runs = [(chip * CORES + core) * run for chip in range(chips)]
                    hidden = [hidden_ref[at : at + run, low : low + TURN] for at in runs]
                    signed = jnp.concatenate(hidden) * sign
                    turned = jnp.dot(signed, table, preferred_element_type=F32).astype(BF16)
                    for piece in range(0, TURN, LANES):
                        part, inside = divmod(low + piece, half)
                        lanes = slice(inside, inside + LANES)
                        value = turned[:, piece : piece + LANES]
                        if part == keep:
                            same_refs[core][:, lanes] = value
                        else:
                            at = core * chips * run
                            other_vmem[at : at + chips * run, lanes] = value
                for piece in range(0, TURN, LANES):
                    part, inside = divmod(low + piece, half)
                    if part != keep:
                        lanes = pl.ds(inside, LANES)
                        copy = pltpu.make_async_copy(
                            other_vmem.at[:, lanes], other_ref.at[:, lanes], sems.at[inside // LANES]
                        )
                        copy.start()
                        copies.append(copy)
            for copy in copies:
                copy.wait()


def turn(hidden, sign_bits):
    rows, width = hidden.shape
    table = (sylvester(TURN) * (1.0 / 16.0)).astype(BF16)
    whole = jax.ShapeDtypeStruct((rows, width // PARTS), BF16)
    block = jax.ShapeDtypeStruct((rows // CORES, width // PARTS), BF16)
    vmem = pl.BlockSpec(memory_space=pltpu.VMEM)
    return pl.pallas_call(
        turn_kernel,
        out_shape=[block, block, whole],
        out_specs=[vmem, vmem, pl.BlockSpec(memory_space=pl.ANY)],
        scratch_shapes=[
            pltpu.VMEM(whole.shape, BF16),
            pltpu.SemaphoreType.DMA((width // PARTS // LANES,)),
        ],
        cost_estimate=pl.CostEstimate(
            flops=2 * rows * width * TURN, bytes_accessed=4 * rows * width, transcendentals=0
        ),
        compiler_params=params(24),
    )(hidden, sign_bits.reshape(1, width), table)


def project_kernel(rows, give, *refs):
    (*act_refs, mixed_ref, out_ref, weight_vmem) = refs
    for y in range(mixed_ref.shape[0]):
        for side in range(2):
            weight_vmem[y * rows : (y + 1) * rows, side * LANES : (side + 1) * LANES] = mixed_ref[
                y, side * rows : (side + 1) * rows
            ]
    same, beside, across, corner = act_refs[0:2], act_refs[2], act_refs[3:5], act_refs[5]
    x, core = lax.axis_index("x"), lax.axis_index("core")
    count = out_ref.shape[1]
    for half in range(CORES):

        @pl.when(jnp.bitwise_xor(core, give) == half)
        def _(half=half):
            at = slice(half * count, (half + 1) * count)
            acts = same[half][...], beside[at], across[half][...], corner[at]
            for flip, act in enumerate(acts):
                value = jnp.dot(act, weight_vmem[...], preferred_element_type=F32)
                out_ref[jnp.bitwise_xor(x, flip)] = value.astype(out_ref.dtype)


def project(acts, mixed, rows, give):
    count, half = acts[0].shape
    groups = PARTS * SIDES
    return pl.pallas_call(
        lambda *refs: project_kernel(rows, give, *refs),
        out_shape=jax.ShapeDtypeStruct((groups, count, 2 * LANES), BF16 if give else F32),
        scratch_shapes=[pltpu.VMEM((half, 2 * LANES), BF16)],
        cost_estimate=pl.CostEstimate(
            flops=groups * 4 * count * half * LANES,
            bytes_accessed=groups * 2 * count * half,
            transcendentals=0,
        ),
        compiler_params=params(24),
    )(*acts, mixed)


def total_kernel(parts_ref, out_ref):
    sides, parts, chips, _, width = parts_ref.shape
    for side in range(sides):
        total = None
        for part in range(parts):
            for chip in range(chips):
                value = parts_ref[side, part, chip].astype(F32)
                total = value if total is None else total + value
        out_ref[:, side * width : (side + 1) * width] = total.astype(BF16)


def total(parts):
    sides, _, _, rows, width = parts.shape
    return pl.pallas_call(
        total_kernel,
        out_shape=jax.ShapeDtypeStruct((rows, sides * width), BF16),
        cost_estimate=pl.CostEstimate(
            flops=parts.size, bytes_accessed=2 * parts.size, transcendentals=0
        ),
        compiler_params=params(24),
    )(parts)


def swap(block, flip):
    return lax.ppermute(block, "x", [(x, x ^ flip) for x in range(lax.axis_size("x"))])


def per_device(hidden, codes, scales, sign_bits):
    row_count, local_width = hidden.shape
    x_count, far_count = lax.axis_size("x"), lax.axis_size("far")
    tp_count = lax.axis_size("z") * lax.axis_size("core")
    rows = local_width // PARTS // (far_count * lax.axis_size("near"))
    padded = -(-2 * rows // (STEP * tp_count)) * STEP * tp_count

    weight = weight_share(codes, scales, rows, padded)
    pieces = weight.reshape(tp_count, padded // tp_count, LANES)
    pieces = lax.all_to_all(pieces, ("z", "core"), 0, 0, tiled=True)

    same0, same1, other = turn(hidden, sign_bits)
    pieces = lax.optimization_barrier((pieces, other))[0]
    beside, corner = swap(other, 1), swap(other, PARTS + 1)
    across = swap(same0, PARTS), swap(same1, PARTS)

    near_count = lax.axis_size("near")
    mixed = mix(pieces.reshape(padded, LANES), tp_count, near_count)
    mixed = mixed.reshape(near_count * tp_count, padded // tp_count, LANES)
    mixed = lax.all_to_all(mixed, ("near", "z", "core"), 0, 0, tiled=True)
    mixed = mixed.reshape(near_count, padded, LANES)[:, : 2 * rows]
    mixed = lax.all_gather(mixed, "far", tiled=True)

    acts = [same0, same1, beside, *across, corner]
    give = project(acts, mixed, rows, 1)
    got = lax.ppermute(give, "core", [(0, 1), (1, 0)])
    chip_sum = (project(acts, mixed, rows, 0) + got.astype(F32)).astype(BF16)
    out_rows = row_count // tp_count
    blocks = x_count * lax.axis_size("z")
    parts = chip_sum.reshape(blocks, out_rows, 2 * LANES)
    parts = lax.all_to_all(parts, ("x", "z"), 0, 0, tiled=True)
    return total(parts.reshape(SIDES, PARTS, -1, out_rows, 2 * LANES))


def solution(mesh):
    devices = mesh.devices.reshape(4, 4, 2, 8, 2)
    grid = Mesh(devices, ("x", "far", "near", "z", "core"))
    rep, tp = ("x", "far", "near"), ("z", "core")
    return jax.shard_map(
        per_device,
        mesh=grid,
        in_specs=(P(rep, tp), P(tp, None), P(tp, None), P(tp)),
        out_specs=P(rep + tp, None),
        check_vma=False,
    )
```
